32 devices in a mesh: ao: 4 (over z), fit: 8 (over y, x, core).
Axes of the slice: x: 2, y: 2, z: 4, core: 2. Of those that a mesh axis runs over, the one named last changes fastest.
Arguments:
- coefficients: bfloat16 [512, 128], P('ao'), may hold values from -2 to 2
- three_center: bfloat16 [32, 512, 4096], P('fit', 'ao'), may hold values from -0.09375 to 0.09375
- pair_blocks: int32 [4, 32], P('ao'), may hold values from 0 to 3
- pair_count: int32 [4], P('ao'), may hold values from 1 to 32, as said below
Outputs:
- exchange: float32 [512, 512], P('ao', 'fit')
The draws below stay inside these ranges and needn't reach their ends.
Inputs may be any that keep to these rules, and one draw needn't show every extreme that they name: Row block m uses its first pair_count[m] slots; some row block has all 32 live in every draw.
All inputs are finite; a program needn't handle non-finite values.
Results may differ from the reference program's by a relative error of at most 0.0012.
Values may be sent and summed in bfloat16 or wider, within the bound.
No kernel may reach another device: no remote copies, remote signals or barrier semaphores. Data moves between devices by JAX's collectives and lax.ppermute only.
A program may use at most 64 MiB of HBM per device.

```python
import jax
import jax.numpy as jnp
from jax import lax

BLK = 128
OCC = 128
PAIRS = 32
NBLK = 4
NAO = 512
FIT = 32


def draw_pair_count(key, part):
    key = jax.random.fold_in(key, 7)
    first, second = jax.random.split(key)
    divisor = jax.random.randint(first, (NBLK,), 1, 9)
    counts = jnp.maximum(PAIRS // divisor, 1)
    where_full = jax.random.randint(second, (), 0, NBLK)
    return counts.at[where_full].set(PAIRS).astype(jnp.int32)


def place_ends(drawn, stream_key, low, largest):
    spot = [jax.random.randint(jax.random.fold_in(stream_key, axis), (), 0, length) for axis, length in enumerate(drawn.shape)]
    widest = drawn.shape.index(max(drawn.shape))
    neighbour = spot[:widest] + [(spot[widest] + 1) % drawn.shape[widest]] + spot[widest + 1:]
    return drawn.at[tuple(spot)].set(low).at[tuple(neighbour)].set(largest)


def steps_of(key, dims, cuts, low, top_value):
    loudness = 1.0
    for axis_at, shards_of in cuts:
        draws = jax.random.uniform(jax.random.fold_in(jax.random.fold_in(key, 6), axis_at), (shards_of,), jnp.float32, low / len(cuts), top_value / len(cuts))
        loudness = loudness * jnp.repeat(jnp.exp(draws), dims[axis_at] // shards_of).reshape((-1,) + (1,) * (len(dims) - 1 - axis_at))
    return loudness


def scatter_about(stream_key, shape, spread, bound, cuts=(), kind=jnp.bfloat16):
    gain = steps_of(stream_key, shape, cuts, -0.22, 0.18) if cuts else 1.0
    values = jax.random.normal(stream_key, shape, jnp.float32) * spread * gain
    return jnp.minimum(jnp.maximum(values, -bound), bound).astype(kind)


def setup_inputs(seed: int = 0) -> dict:
    arg_keys = jax.random.split(jax.random.key(seed), 5)
    return {
        "coefficients": scatter_about(arg_keys[0], (NAO, OCC), ((FIT * OCC) ** -0.25), 2.0, ((0, 4),)),
        "three_center": scatter_about(arg_keys[1], (FIT, NAO, PAIRS * BLK), (PAIRS * BLK) ** -0.5, 0.09375, ((0, 8), (1, 4))),
        "pair_blocks": place_ends(jax.random.randint(arg_keys[2], (NBLK, PAIRS), 0, NBLK), jax.random.fold_in(arg_keys[2], 1), 0, NBLK - 1).astype(jnp.int32),
        "pair_count": draw_pair_count(jax.random.fold_in(arg_keys[4], 71), 0),
    }


def reference(coefficients, three_center, pair_blocks, pair_count):
    blocks = coefficients.reshape(NBLK, BLK, OCC)

    def one_block(index):
        chosen = blocks[pair_blocks[index]]
        live = (jnp.arange(PAIRS, dtype=jnp.int32) < pair_count[index])[:, None, None]
        chosen = jnp.where(live, chosen, jnp.zeros_like(chosen)).reshape(PAIRS * BLK, OCC)
        rows = lax.dynamic_slice_in_dim(three_center, (index * BLK).astype(jnp.int32), BLK, 1)
        half = jnp.dot(rows.reshape(FIT * BLK, PAIRS * BLK), chosen, preferred_element_type=jnp.float32)
        half = half.astype(jnp.bfloat16).reshape(FIT, BLK, OCC)
        return half.transpose(1, 0, 2).reshape(BLK, FIT * OCC)

    halves = lax.map(one_block, jnp.arange(NBLK, dtype=jnp.int32))
    flat = halves.reshape(NAO, FIT * OCC).astype(jnp.float32)
    return jnp.dot(flat, flat.T, preferred_element_type=jnp.float32, precision=lax.Precision.HIGHEST)
```

```python
import functools

import jax
import jax.numpy as jnp
from jax import lax
from jax.experimental import pallas as pl
from jax.experimental.pallas import tpu as pltpu
from jax.sharding import PartitionSpec as P

VMEM = pl.BlockSpec(memory_space=pltpu.VMEM)
SMEM = pl.BlockSpec(memory_space=pltpu.SMEM)


def gathered_form(coefficients, three_center, pair_blocks, pair_count):
    fit_dev = three_center.shape[0]
    block = three_center.shape[1]
    pairs = pair_blocks.shape[1]
    orbitals = coefficients.shape[1]
    every = lax.all_gather(coefficients, "ao", axis=0, tiled=True)
    chosen = every.reshape(-1, block, orbitals)[pair_blocks[0]]
    live = (jnp.arange(pairs, dtype=jnp.int32) < pair_count[0])[:, None, None]
    chosen = jnp.where(live, chosen, jnp.zeros_like(chosen)).reshape(pairs * block, orbitals)
    half = jnp.dot(
        three_center.reshape(fit_dev * block, pairs * block),
        chosen,
        preferred_element_type=jnp.float32,
    )
    half = half.astype(jnp.bfloat16).reshape(fit_dev, block, orbitals)
    terms = jnp.einsum(
        "fmi,fni->mn",
        half,
        lax.all_gather(half, "ao", axis=1, tiled=True),
        preferred_element_type=jnp.float32,
    )
    return lax.psum_scatter(terms, "fit", scatter_dimension=1, tiled=True)


def slot_sums(blocks, pairs, width, pair_ref, count_ref, x_ref, sums_ref, acc):
    z = lax.axis_index("ao")
    acc[...] = jnp.zeros_like(acc)

    def add(p, carry):
        place = pair_ref[0, p] ^ z
        acc[place] += x_ref[0, :, pl.ds(pl.multiple_of(p * width, width), width)].astype(jnp.float32)
        return carry

    lax.fori_loop(0, jnp.minimum(count_ref[0], pairs), add, 0)
    for b in range(blocks):
        whole = acc[b]
        high = whole.astype(jnp.bfloat16)
        sums_ref[:, b * width : (b + 1) * width] = high
        sums_ref[:, (blocks + b) * width : (blocks + b + 1) * width] = (whole - high.astype(jnp.float32)).astype(jnp.bfloat16)


def transform(blocks, sums_ref, *refs):
    half_ref = refs[-1]
    coefficients = jnp.concatenate([ref[...] for ref in refs[:-1]] * 2, axis=0)
    half = jnp.dot(sums_ref[...], coefficients, preferred_element_type=jnp.float32)
    half_ref[...] = half.astype(jnp.bfloat16).reshape(half_ref.shape)


def products(blocks, fits, *refs):
    halves, keep_ref, send_ref, whole = refs[:blocks], refs[blocks], refs[blocks + 1], refs[blocks + 2]
    z, f = lax.axis_index("ao"), lax.axis_index("fit")
    q, core = f // 2, f % 2
    columns = keep_ref.shape[1]
    for k in range(blocks):
        total = None
        for p in range(fits):
            term = lax.dot_general(
                halves[k][p], halves[0][p], (((1,), (1,)), ((), ())), preferred_element_type=jnp.float32
            )
            total = term if total is None else total + term
        whole[k] = total
    for k in range(blocks):
        place = z ^ q ^ k
        keep_ref[place] = whole[k, pl.ds(pl.multiple_of(core * columns, columns), columns), :]
        send_ref[place] = whole[k, pl.ds(pl.multiple_of((1 - core) * columns, columns), columns), :]


def finish(own_ref, *refs):
    out_ref = refs[-1]
    total = own_ref[...]
    for ref in refs[:-1]:
        total = total + ref[...]
    out_ref[...] = total.T


def permuted_form(blocks, coefficients, three_center, pair_blocks, pair_count):
    fits, block, wide = three_center.shape
    pairs = pair_blocks.shape[1]
    orbitals = coefficients.shape[1]
    columns = block // 2
    chips = range(1, blocks)

    def over_ao(x):
        return [lax.ppermute(x, "ao", [(i, i ^ k) for i in range(blocks)]) for k in chips]

    def over_fit(x, k):
        return lax.ppermute(x, "fit", [(i, i ^ k) for i in range(2 * blocks)])

    coefs = [coefficients] + over_ao(coefficients)
    sums = pl.pallas_call(
        functools.partial(slot_sums, blocks, pairs, block),
        grid=(fits,),
        out_shape=jax.ShapeDtypeStruct((fits * block, 2 * blocks * block), jnp.bfloat16),
        in_specs=[SMEM, SMEM, pl.BlockSpec((1, block, wide), lambda i: (i, 0, 0))],
        out_specs=pl.BlockSpec((block, 2 * blocks * block), lambda i: (i, 0)),
        scratch_shapes=[pltpu.VMEM((blocks, block, block), jnp.float32)],
        name="slot_sums",
    )(pair_blocks, pair_count, three_center)
    half = pl.pallas_call(
        functools.partial(transform, blocks),
        out_shape=jax.ShapeDtypeStruct((fits, block, orbitals), jnp.bfloat16),
        in_specs=[VMEM] * (blocks + 1),
        out_specs=VMEM,
        name="transform",
    )(sums, *coefs)
    halves = [half] + over_ao(half)
    piece = jax.ShapeDtypeStruct((blocks, columns, block), jnp.float32)
    keep, send = pl.pallas_call(
        functools.partial(products, blocks, fits),
        out_shape=(piece, piece),
        in_specs=[VMEM] * blocks,
        out_specs=(VMEM, VMEM),
        scratch_shapes=[pltpu.VMEM((blocks, block, block), jnp.float32)],
        name="products",
    )(*halves)
    chip = keep + over_fit(send, 1)
    parts = [chip[0]] + [over_fit(chip[k], 2 * k) for k in chips]
    return pl.pallas_call(
        finish,
        out_shape=jax.ShapeDtypeStruct((block, columns), jnp.float32),
        in_specs=[VMEM] * blocks,
        out_specs=VMEM,
        name="finish",
    )(*parts)


def solution(mesh):
    blocks, fit = mesh.shape["ao"], mesh.shape["fit"]

    def per_device(coefficients, three_center, pair_blocks, pair_count):
        block = three_center.shape[1]
        fast = (
            fit == 2 * blocks
            and blocks & (blocks - 1) == 0
            and 1 < blocks <= 4
            and block % 128 == 0
            and coefficients.shape[1] % 128 == 0
            and coefficients.shape[0] == block
            and pair_blocks.shape[0] == 1
        )
        form = functools.partial(permuted_form, blocks) if fast else gathered_form
        return form(coefficients, three_center, pair_blocks, pair_count)

    return jax.shard_map(
        per_device,
        mesh=mesh,
        in_specs=(P("ao", None), P("fit", "ao", None), P("ao", None), P("ao")),
        out_specs=P("ao", "fit"),
        check_vma=False,
    )
```

```python
import functools

import jax
import jax.numpy as jnp
from jax import lax
from jax.experimental import pallas as pl
from jax.experimental.pallas import tpu as pltpu
from jax.sharding import PartitionSpec as P

VMEM = pl.BlockSpec(memory_space=pltpu.VMEM)
HBM = pl.BlockSpec(memory_space=pltpu.HBM)
SMEM = pl.BlockSpec(memory_space=pltpu.SMEM)
TOGETHER = 4


def gathered_form(coefficients, three_center, pair_blocks, pair_count):
    fit_dev = three_center.shape[0]
    block = three_center.shape[1]
    pairs = pair_blocks.shape[1]
    orbitals = coefficients.shape[1]
    every = lax.all_gather(coefficients, "ao", axis=0, tiled=True)
    chosen = every.reshape(-1, block, orbitals)[pair_blocks[0]]
    live = (jnp.arange(pairs, dtype=jnp.int32) < pair_count[0])[:, None, None]
    chosen = jnp.where(live, chosen, jnp.zeros_like(chosen)).reshape(pairs * block, orbitals)
    half = jnp.dot(
        three_center.reshape(fit_dev * block, pairs * block),
        chosen,
        preferred_element_type=jnp.float32,
    )
    half = half.astype(jnp.bfloat16).reshape(fit_dev, block, orbitals)
    terms = jnp.einsum(
        "fmi,fni->mn",
        half,
        lax.all_gather(half, "ao", axis=1, tiled=True),
        preferred_element_type=jnp.float32,
    )
    return lax.psum_scatter(terms, "fit", scatter_dimension=1, tiled=True)


def slot_sums(blocks, pair_ref, count_ref, x_ref, sums_ref, buffer, arrived, pairs_here, listed, order, counts):
    fits, block, wide = x_ref.shape
    pairs = pair_ref.shape[1]
    slots = pltpu.make_async_copy(pair_ref, pairs_here, listed)
    slots.start()
    copies = [
        pltpu.make_async_copy(x_ref.at[i], buffer.at[i, :, pl.ds(0, wide)], arrived.at[i]) for i in range(fits)
    ]
    for copy in copies:
        copy.start()
    buffer[:, :, wide:] = jnp.zeros((fits, block, block), buffer.dtype)
    z = lax.axis_index("ao")
    for place in range(blocks):
        counts[place] = 0
    slots.wait()

    def enlist(p, carry):
        place = pairs_here[0, p] ^ z
        n = counts[place]
        order[place, n] = p
        counts[place] = n + 1
        return carry

    lax.fori_loop(0, jnp.minimum(count_ref[0], pairs), enlist, 0)
    for place in range(blocks):
        n = counts[place]
        for j in range(TOGETHER - 1):
            order[place, n + j] = pairs
    for i in range(fits):
        copies[i].wait()
        for place in range(blocks):

            def slot(s):
                start = pl.multiple_of(order[place, s] * block, block)
                return buffer[i, :, pl.ds(start, block)].astype(jnp.float32)

            def add(s, total):
                s = s * TOGETHER
                return total + ((slot(s) + slot(s + 1)) + (slot(s + 2) + slot(s + 3)))

            rounds = (counts[place] + TOGETHER - 1) // TOGETHER
            whole = lax.fori_loop(0, rounds, add, jnp.zeros((block, block), jnp.float32))
            high = whole.astype(jnp.bfloat16)
            low = (whole - high.astype(jnp.float32)).astype(jnp.bfloat16)
            rows = slice(i * block, (i + 1) * block)
            sums_ref[rows, place * block : (place + 1) * block] = high
            sums_ref[rows, (blocks + place) * block : (blocks + place + 1) * block] = low


def transform(blocks, sums_ref, *refs):
    half_ref = refs[-1]
    coefficients = jnp.concatenate([ref[...] for ref in refs[:-1]] * 2, axis=0)
    half = jnp.dot(sums_ref[...], coefficients, preferred_element_type=jnp.float32)
    half_ref[...] = half.astype(jnp.bfloat16).reshape(half_ref.shape)


def products(blocks, fits, *refs):
    halves, keep_ref, send_ref, whole = refs[:blocks], refs[blocks], refs[blocks + 1], refs[blocks + 2]
    z, f = lax.axis_index("ao"), lax.axis_index("fit")
    q, core = f // 2, f % 2
    columns = keep_ref.shape[1]
    for k in range(blocks):
        total = None
        for p in range(fits):
            term = lax.dot_general(
                halves[k][p], halves[0][p], (((1,), (1,)), ((), ())), preferred_element_type=jnp.float32
            )
            total = term if total is None else total + term
        whole[k] = total
    for k in range(blocks):
        place = z ^ q ^ k
        keep_ref[place] = whole[k, pl.ds(pl.multiple_of(core * columns, columns), columns), :]
        send_ref[place] = whole[k, pl.ds(pl.multiple_of((1 - core) * columns, columns), columns), :]


def permuted_form(blocks, coefficients, three_center, pair_blocks, pair_count):
    fits, block, wide = three_center.shape
    pairs = pair_blocks.shape[1]
    orbitals = coefficients.shape[1]
    columns = block // 2
    chips = range(1, blocks)

    def over_ao(x):
        return [lax.ppermute(x, "ao", [(i, i ^ k) for i in range(blocks)]) for k in chips]

    def over_fit(x, k):
        return lax.ppermute(x, "fit", [(i, i ^ k) for i in range(2 * blocks)])

    def held(x):
        return pltpu.with_memory_space_constraint(x, pltpu.VMEM)

    def far(x):
        return pltpu.with_memory_space_constraint(x, pltpu.HBM)

    coefs = [coefficients] + over_ao(coefficients)
    sums = pl.pallas_call(
        functools.partial(slot_sums, blocks),
        out_shape=pltpu.VMEM((fits * block, 2 * blocks * block), jnp.bfloat16),
        in_specs=[HBM, SMEM, HBM],
        out_specs=VMEM,
        scratch_shapes=[
            pltpu.VMEM((fits, block, wide + block), jnp.bfloat16),
            pltpu.SemaphoreType.DMA((fits,)),
            pltpu.SMEM((1, pairs), jnp.int32),
            pltpu.SemaphoreType.DMA,
            pltpu.SMEM((blocks, pairs + TOGETHER), jnp.int32),
            pltpu.SMEM((blocks,), jnp.int32),
        ],
        compiler_params=pltpu.CompilerParams(vmem_limit_bytes=32 << 20),
        name="slot_sums",
    )(far(pair_blocks), pair_count, far(three_center))
    half = pl.pallas_call(
        functools.partial(transform, blocks),
        out_shape=pltpu.VMEM((fits, block, orbitals), jnp.bfloat16),
        in_specs=[VMEM] * (blocks + 1),
        out_specs=VMEM,
        name="transform",
    )(held(sums), *[held(x) for x in coefs])
    halves = [half] + over_ao(half)
    piece = pltpu.VMEM((blocks, columns, block), jnp.float32)
    keep, send = pl.pallas_call(
        functools.partial(products, blocks, fits),
        out_shape=(piece, piece),
        in_specs=[VMEM] * blocks,
        out_specs=(VMEM, VMEM),
        scratch_shapes=[pltpu.VMEM((blocks, block, block), jnp.float32)],
        name="products",
    )(*[held(x) for x in halves])
    chip = keep + over_fit(send, 1)
    total = chip[0]
    for k in chips:
        total = total + over_fit(chip[k], 2 * k)
    return total.T


def solution(mesh):
    blocks, fit = mesh.shape["ao"], mesh.shape["fit"]

    def per_device(coefficients, three_center, pair_blocks, pair_count):
        block = three_center.shape[1]
        fast = (
            fit == 2 * blocks
            and blocks & (blocks - 1) == 0
            and 1 < blocks <= 4
            and block % 128 == 0
            and coefficients.shape[1] % 128 == 0
            and coefficients.shape[0] == block
            and pair_blocks.shape[0] == 1
        )
        form = functools.partial(permuted_form, blocks) if fast else gathered_form
        return form(coefficients, three_center, pair_blocks, pair_count)

    return jax.shard_map(
        per_device,
        mesh=mesh,
        in_specs=(P("ao", None), P("fit", "ao", None), P("ao", None), P("ao")),
        out_specs=P("ao", "fit"),
        check_vma=False,
    )
```

```python
import functools

import jax
import jax.numpy as jnp
from jax import lax
from jax.experimental import pallas as pl
from jax.experimental.pallas import tpu as pltpu
from jax.sharding import PartitionSpec as P

VMEM = pl.BlockSpec(memory_space=pltpu.VMEM)
HBM = pl.BlockSpec(memory_space=pltpu.HBM)
SMEM = pl.BlockSpec(memory_space=pltpu.SMEM)
TOGETHER = 4
ROUNDS = (
    (4, 3, 0, 1, 5, 9, 13, 6, 11, 10, 2, 8, 15, 14, 12, 7),
    (12, 0, 4, 8, 9, 13, 5, 1, 10, 2, 14, 6, 7, 3, 15, 11),
    (8, 2, 12, 0, 7, 1, 4, 5, 9, 14, 6, 10, 11, 15, 13, 3),
)


def gathered_form(coefficients, three_center, pair_blocks, pair_count):
    fit_dev = three_center.shape[0]
    block = three_center.shape[1]
    pairs = pair_blocks.shape[1]
    orbitals = coefficients.shape[1]
    every = lax.all_gather(coefficients, "ao", axis=0, tiled=True)
    chosen = every.reshape(-1, block, orbitals)[pair_blocks[0]]
    live = (jnp.arange(pairs, dtype=jnp.int32) < pair_count[0])[:, None, None]
    chosen = jnp.where(live, chosen, jnp.zeros_like(chosen)).reshape(pairs * block, orbitals)
    half = jnp.dot(
        three_center.reshape(fit_dev * block, pairs * block),
        chosen,
        preferred_element_type=jnp.float32,
    )
    half = half.astype(jnp.bfloat16).reshape(fit_dev, block, orbitals)
    terms = jnp.einsum(
        "fmi,fni->mn",
        half,
        lax.all_gather(half, "ao", axis=1, tiled=True),
        preferred_element_type=jnp.float32,
    )
    return lax.psum_scatter(terms, "fit", scatter_dimension=1, tiled=True)


def slot_sums(blocks, pair_ref, count_ref, x_ref, sums_ref, buffer, arrived, pairs_here, listed, order, counts):
    fits, block, wide = x_ref.shape
    pairs = pair_ref.shape[1]
    slots = pltpu.make_async_copy(pair_ref, pairs_here, listed)
    slots.start()
    copies = [
        pltpu.make_async_copy(x_ref.at[i], buffer.at[i, :, pl.ds(0, wide)], arrived.at[i]) for i in range(fits)
    ]
    for copy in copies:
        copy.start()
    buffer[:, :, wide:] = jnp.zeros((fits, block, block), buffer.dtype)
    z = lax.axis_index("ao")
    for place in range(blocks):
        counts[place] = 0
    slots.wait()

    def enlist(p, carry):
        place = pairs_here[0, p] ^ z
        n = counts[place]
        order[place, n] = p
        counts[place] = n + 1
        return carry

    lax.fori_loop(0, jnp.minimum(count_ref[0], pairs), enlist, 0)
    for place in range(blocks):
        n = counts[place]
        for j in range(TOGETHER - 1):
            order[place, n + j] = pairs
    for i in range(fits):
        copies[i].wait()
        for place in range(blocks):

            def slot(s):
                start = pl.multiple_of(order[place, s] * block, block)
                return buffer[i, :, pl.ds(start, block)].astype(jnp.float32)

            def add(s, total):
                s = s * TOGETHER
                return total + ((slot(s) + slot(s + 1)) + (slot(s + 2) + slot(s + 3)))

            rounds = (counts[place] + TOGETHER - 1) // TOGETHER
            whole = lax.fori_loop(0, rounds, add, jnp.zeros((block, block), jnp.float32))
            high = whole.astype(jnp.bfloat16)
            low = (whole - high.astype(jnp.float32)).astype(jnp.bfloat16)
            rows = slice(i * block, (i + 1) * block)
            sums_ref[rows, place * block : (place + 1) * block] = high
            sums_ref[rows, (blocks + place) * block : (blocks + place + 1) * block] = low


def transform(sums_ref, own_ref, near_ref, first_ref, second_ref, half_ref):
    first, second = first_ref[...], second_ref[...]
    even = lax.axis_index("fit") % 2 == 0
    parts = [own_ref[...], near_ref[...], jnp.where(even, second, first), jnp.where(even, first, second)]
    coefficients = jnp.concatenate(parts * 2, axis=0)
    half = jnp.dot(sums_ref[...], coefficients, preferred_element_type=jnp.float32)
    half_ref[...] = half.astype(jnp.bfloat16).reshape(half_ref.shape)


def shares():
    senders = [{to: at for at, to in enumerate(r)} for r in ROUNDS]
    table = []
    for chip in range(16):
        z, j = divmod(chip, 4)
        if z == j:
            table.append((3, 3, 0, 0))
            continue
        came = [divmod(s[chip], 4) for s in senders]
        far = came.index((j, j))
        (left,) = [q for p, q in came if p == z]
        table.append((far, 3, came.index((j, left)), came.index((z, left))))
    return table


def products(one, two, three, own, keep_ref, send_ref, held):
    z, f = lax.axis_index("ao"), lax.axis_index("fit")
    chip, core = z * 4 + f // 2, f % 2
    fits, block, _ = own.shape
    columns = block // 2
    for place, ref in enumerate((one, two, three, own)):
        held[place] = jnp.concatenate([ref[p] for p in range(fits)], axis=1)

    def place(n):
        code = sum(row[n] << (2 * at) for at, row in enumerate(shares()))
        return (jnp.int32(code - (1 << 32) if code >> 31 else code) >> (2 * chip)) & 3

    def product(left, right):
        return lax.dot_general(
            left, right, (((1,), (1,)), ((), ())), preferred_element_type=jnp.float32
        )

    def put(total):
        for side, whole in enumerate((total, total.T)):
            for to, at in ((keep_ref, core), (send_ref, 1 - core)):
                to[side] = jnp.where(at == 0, whole[:columns], whole[columns:])

    first = product(held[place(0)], held[place(1)]) + product(held[place(2)], held[place(3)])

    @pl.when(chip // 4 != chip % 4)
    def _():
        put(first)

    @pl.when(chip // 4 == chip % 4)
    def _():
        put(first + product(held[1], held[1]) + product(held[2], held[2]))


def permuted_form(blocks, coefficients, three_center, pair_blocks, pair_count):
    fits, block, wide = three_center.shape
    pairs = pair_blocks.shape[1]
    orbitals = coefficients.shape[1]
    columns = block // 2

    def over_fit(x, k):
        return lax.ppermute(x, "fit", [(i, i ^ k) for i in range(2 * blocks)])

    def held(x):
        return pltpu.with_memory_space_constraint(x, pltpu.VMEM)

    def far(x):
        return pltpu.with_memory_space_constraint(x, pltpu.HBM)

    def device(z, f):
        return z * 2 * blocks + f

    split = [
        (device(z, f), device(z ^ (blocks - 1 - f % 2), f)) for z in range(blocks) for f in range(2 * blocks)
    ]
    first = lax.ppermute(coefficients, ("ao", "fit"), split)
    near = lax.ppermute(coefficients, "ao", [(i, i ^ 1) for i in range(blocks)])
    sums = pl.pallas_call(
        functools.partial(slot_sums, blocks),
        out_shape=pltpu.VMEM((fits * block, 2 * blocks * block), jnp.bfloat16),
        in_specs=[HBM, SMEM, HBM],
        out_specs=VMEM,
        scratch_shapes=[
            pltpu.VMEM((fits, block, wide + block), jnp.bfloat16),
            pltpu.SemaphoreType.DMA((fits,)),
            pltpu.SMEM((1, pairs), jnp.int32),
            pltpu.SemaphoreType.DMA,
            pltpu.SMEM((blocks, pairs + TOGETHER), jnp.int32),
            pltpu.SMEM((blocks,), jnp.int32),
        ],
        compiler_params=pltpu.CompilerParams(vmem_limit_bytes=32 << 20),
        cost_estimate=pl.CostEstimate(
            flops=fits * block * wide, bytes_accessed=2 * fits * block * wide, transcendentals=0
        ),
        name="slot_sums",
    )(far(pair_blocks), pair_count, far(three_center))
    first, sums = lax.optimization_barrier((first, sums))
    coefs = [coefficients, near, first, over_fit(first, 1)]
    half = pl.pallas_call(
        transform,
        out_shape=pltpu.VMEM((fits, block, orbitals), jnp.bfloat16),
        in_specs=[VMEM] * (blocks + 1),
        out_specs=VMEM,
        name="transform",
    )(held(sums), *[held(x) for x in coefs])
    received = [
        lax.ppermute(
            half, ("ao", "fit"), [(2 * at + c, 2 * to + c) for at, to in enumerate(r) for c in range(2)]
        )
        for r in ROUNDS
    ]
    piece = pltpu.VMEM((2, columns, block), jnp.float32)
    keep, send = pl.pallas_call(
        products,
        out_shape=(piece, piece),
        in_specs=[VMEM] * 4,
        out_specs=(VMEM, VMEM),
        scratch_shapes=[pltpu.VMEM((4, block, fits * orbitals), jnp.bfloat16)],
        name="products",
    )(*[held(x) for x in received + [half]])
    chip = keep + over_fit(send, 1)
    across = [
        (device(z, 2 * j + c), device(j, 2 * z + c))
        for z in range(blocks)
        for j in range(blocks)
        for c in range(2)
        if z != j
    ]
    return (chip[0] + lax.ppermute(chip[1], ("ao", "fit"), across)).T


def solution(mesh):
    blocks, fit = mesh.shape["ao"], mesh.shape["fit"]

    def per_device(coefficients, three_center, pair_blocks, pair_count):
        block = three_center.shape[1]
        fast = (
            fit == 2 * blocks
            and blocks == 4
            and block % 128 == 0
            and coefficients.shape[1] % 128 == 0
            and coefficients.shape[0] == block
            and pair_blocks.shape[0] == 1
        )
        form = functools.partial(permuted_form, blocks) if fast else gathered_form
        return form(coefficients, three_center, pair_blocks, pair_count)

    return jax.shard_map(
        per_device,
        mesh=mesh,
        in_specs=(P("ao", None), P("fit", "ao", None), P("ao", None), P("ao")),
        out_specs=P("ao", "fit"),
        check_vma=False,
    )
```

```python
import functools

import jax
import jax.numpy as jnp
from jax import lax
from jax.experimental import pallas as pl
from jax.experimental.pallas import tpu as pltpu
from jax.sharding import PartitionSpec as P

VMEM = pl.BlockSpec(memory_space=pltpu.VMEM)
HBM = pl.BlockSpec(memory_space=pltpu.HBM)
SMEM = pl.BlockSpec(memory_space=pltpu.SMEM)
TOGETHER = 4
REDUCE = (
    (0, 1, 2, 6, 4, 5, 3, 7, 8, 12, 10, 11, 9, 13, 14, 15),
    (1, 6, 0, 2, 7, 4, 5, 3, 10, 8, 11, 12, 15, 14, 13, 9),
    (6, 2, 1, 0, 5, 3, 7, 4, 12, 11, 8, 10, 13, 15, 9, 14),
    (2, 0, 6, 1, 3, 7, 4, 5, 11, 10, 12, 8, 14, 9, 15, 13),
)


def gathered_form(coefficients, three_center, pair_blocks, pair_count):
    fit_dev = three_center.shape[0]
    block = three_center.shape[1]
    pairs = pair_blocks.shape[1]
    orbitals = coefficients.shape[1]
    every = lax.all_gather(coefficients, "ao", axis=0, tiled=True)
    chosen = every.reshape(-1, block, orbitals)[pair_blocks[0]]
    live = (jnp.arange(pairs, dtype=jnp.int32) < pair_count[0])[:, None, None]
    chosen = jnp.where(live, chosen, jnp.zeros_like(chosen)).reshape(pairs * block, orbitals)
    half = jnp.dot(
        three_center.reshape(fit_dev * block, pairs * block),
        chosen,
        preferred_element_type=jnp.float32,
    )
    half = half.astype(jnp.bfloat16).reshape(fit_dev, block, orbitals)
    terms = jnp.einsum(
        "fmi,fni->mn",
        half,
        lax.all_gather(half, "ao", axis=1, tiled=True),
        preferred_element_type=jnp.float32,
    )
    return lax.psum_scatter(terms, "fit", scatter_dimension=1, tiled=True)


def slot_sums(blocks, pair_ref, count_ref, x_ref, sums_ref, buffer, arrived, pairs_here, listed, order, counts):
    fits, block, wide = x_ref.shape
    pairs = pair_ref.shape[1]
    slots = pltpu.make_async_copy(pair_ref, pairs_here, listed)
    slots.start()
    copies = [
        pltpu.make_async_copy(x_ref.at[i], buffer.at[i, :, pl.ds(0, wide)], arrived.at[i]) for i in range(fits)
    ]
    for copy in copies:
        copy.start()
    buffer[:, :, wide:] = jnp.zeros((fits, block, block), buffer.dtype)
    z = lax.axis_index("ao")
    for place in range(blocks):
        counts[place] = 0
    slots.wait()

    def enlist(p, carry):
        place = pairs_here[0, p] ^ z
        n = counts[place]
        order[place, n] = p
        counts[place] = n + 1
        return carry

    lax.fori_loop(0, jnp.minimum(count_ref[0], pairs), enlist, 0)
    for place in range(blocks):
        n = counts[place]
        for j in range(TOGETHER - 1):
            order[place, n + j] = pairs
    for i in range(fits):
        copies[i].wait()
        for place in range(blocks):

            def slot(s):
                start = pl.multiple_of(order[place, s] * block, block)
                return buffer[i, :, pl.ds(start, block)].astype(jnp.float32)

            def add(s, total):
                s = s * TOGETHER
                return total + ((slot(s) + slot(s + 1)) + (slot(s + 2) + slot(s + 3)))

            rounds = (counts[place] + TOGETHER - 1) // TOGETHER
            whole = lax.fori_loop(0, rounds, add, jnp.zeros((block, block), jnp.float32))
            high = whole.astype(jnp.bfloat16)
            low = (whole - high.astype(jnp.float32)).astype(jnp.bfloat16)
            rows = slice(i * block, (i + 1) * block)
            sums_ref[rows, place * block : (place + 1) * block] = high
            sums_ref[rows, (blocks + place) * block : (blocks + place + 1) * block] = low


def transform(sums_ref, own_ref, third_ref, second_ref, near_ref, half_ref):
    parts = [own_ref[...], near_ref[...], second_ref[...], third_ref[...]]
    coefficients = jnp.concatenate(parts * 2, axis=0)
    half = jnp.dot(sums_ref[...], coefficients, preferred_element_type=jnp.float32)
    half_ref[...] = half.astype(jnp.bfloat16).reshape(half_ref.shape)


def blocks_sent():
    codes = []
    for targets in REDUCE:
        code = 0
        for chip, to in enumerate(targets):
            z = chip // 4
            code |= ((to % 4) ^ z if to // 4 == z else 3) << (2 * chip)
        codes.append(code - (1 << 32) if code >> 31 else code)
    return codes


def products(near, own, far, keep_ref, send_ref, whole):
    z, f = lax.axis_index("ao"), lax.axis_index("fit")
    chip, core = z * 4 + f // 2, f % 2
    columns = keep_ref.shape[1]

    def rows(ref):
        return jnp.concatenate([ref[p] for p in range(ref.shape[0])], axis=1)

    mine, next_to, beyond = rows(own), rows(near), rows(far)
    pairs = ((mine, mine), (next_to, mine), (beyond, mine), (beyond, next_to))
    for n, (left, right) in enumerate(pairs):
        whole[n] = lax.dot_general(
            left, right, (((1,), (1,)), ((), ())), preferred_element_type=jnp.float32
        )
    for m, code in enumerate(blocks_sent()):
        n = (jnp.int32(code) >> (2 * chip)) & 3
        keep_ref[m] = whole[n, pl.ds(pl.multiple_of(core * columns, columns), columns), :]
        send_ref[m] = whole[n, pl.ds(pl.multiple_of((1 - core) * columns, columns), columns), :]


def permuted_form(blocks, coefficients, three_center, pair_blocks, pair_count):
    fits, block, wide = three_center.shape
    pairs = pair_blocks.shape[1]
    orbitals = coefficients.shape[1]
    columns = block // 2

    def over_ao(x, k):
        return lax.ppermute(x, "ao", [(i, i ^ k) for i in range(blocks)])

    def over_fit(x, k):
        return lax.ppermute(x, "fit", [(i, i ^ k) for i in range(2 * blocks)])

    def held(x):
        return pltpu.with_memory_space_constraint(x, pltpu.VMEM)

    def far(x):
        return pltpu.with_memory_space_constraint(x, pltpu.HBM)

    coefs = [over_ao(coefficients, k) for k in (3, 2, 1)]
    sums = pl.pallas_call(
        functools.partial(slot_sums, blocks),
        out_shape=pltpu.VMEM((fits * block, 2 * blocks * block), jnp.bfloat16),
        in_specs=[HBM, SMEM, HBM],
        out_specs=VMEM,
        scratch_shapes=[
            pltpu.VMEM((fits, block, wide + block), jnp.bfloat16),
            pltpu.SemaphoreType.DMA((fits,)),
            pltpu.SMEM((1, pairs), jnp.int32),
            pltpu.SemaphoreType.DMA,
            pltpu.SMEM((blocks, pairs + TOGETHER), jnp.int32),
            pltpu.SMEM((blocks,), jnp.int32),
        ],
        compiler_params=pltpu.CompilerParams(vmem_limit_bytes=32 << 20),
        cost_estimate=pl.CostEstimate(
            flops=fits * block * wide, bytes_accessed=2 * fits * block * wide, transcendentals=0
        ),
        name="slot_sums",
    )(far(pair_blocks), pair_count, far(three_center))
    half = pl.pallas_call(
        transform,
        out_shape=pltpu.VMEM((fits, block, orbitals), jnp.bfloat16),
        in_specs=[VMEM] * (blocks + 1),
        out_specs=VMEM,
        name="transform",
    )(held(sums), *[held(x) for x in [coefficients] + coefs])
    near, far_rows = over_ao(half, 1), over_ao(half, 2)
    piece = pltpu.VMEM((blocks, columns, block), jnp.float32)
    keep, send = pl.pallas_call(
        products,
        out_shape=(piece, piece),
        in_specs=[VMEM] * 3,
        out_specs=(VMEM, VMEM),
        scratch_shapes=[pltpu.VMEM((blocks, block, block), jnp.float32)],
        name="products",
    )(held(near), held(half), held(far_rows))
    chip = keep + over_fit(send, 1)
    total = None
    for m, targets in enumerate(REDUCE):
        pairs = [(2 * at + c, 2 * to + c) for at, to in enumerate(targets) for c in range(2)]
        part = lax.ppermute(chip[m], ("ao", "fit"), pairs)
        total = part if total is None else total + part
    return total.T


def solution(mesh):
    blocks, fit = mesh.shape["ao"], mesh.shape["fit"]

    def per_device(coefficients, three_center, pair_blocks, pair_count):
        block = three_center.shape[1]
        fast = (
            fit == 2 * blocks
            and blocks == 4
            and block % 128 == 0
            and coefficients.shape[1] % 128 == 0
            and coefficients.shape[0] == block
            and pair_blocks.shape[0] == 1
        )
        form = functools.partial(permuted_form, blocks) if fast else gathered_form
        return form(coefficients, three_center, pair_blocks, pair_count)

    return jax.shard_map(
        per_device,
        mesh=mesh,
        in_specs=(P("ao", None), P("fit", "ao", None), P("ao", None), P("ao")),
        out_specs=P("ao", "fit"),
        check_vma=False,
    )
```

```python
import functools

import jax
import jax.numpy as jnp
from jax import lax
from jax.experimental import pallas as pl
from jax.experimental.pallas import tpu as pltpu
from jax.sharding import PartitionSpec as P

VMEM = pl.BlockSpec(memory_space=pltpu.VMEM)
HBM = pl.BlockSpec(memory_space=pltpu.HBM)
SMEM = pl.BlockSpec(memory_space=pltpu.SMEM)
TOGETHER = 4
REDUCE = (
    (0, 2, 6, 1, 4, 7, 3, 5, 12, 8, 10, 11, 13, 9, 15, 14),
    (1, 0, 2, 6, 3, 5, 4, 7, 11, 10, 12, 8, 14, 13, 9, 15),
    (6, 1, 0, 2, 5, 3, 7, 4, 10, 11, 8, 12, 15, 14, 13, 9),
    (2, 6, 1, 0, 7, 4, 5, 3, 8, 12, 11, 10, 9, 15, 14, 13),
)


def gathered_form(coefficients, three_center, pair_blocks, pair_count):
    fit_dev = three_center.shape[0]
    block = three_center.shape[1]
    pairs = pair_blocks.shape[1]
    orbitals = coefficients.shape[1]
    every = lax.all_gather(coefficients, "ao", axis=0, tiled=True)
    chosen = every.reshape(-1, block, orbitals)[pair_blocks[0]]
    live = (jnp.arange(pairs, dtype=jnp.int32) < pair_count[0])[:, None, None]
    chosen = jnp.where(live, chosen, jnp.zeros_like(chosen)).reshape(pairs * block, orbitals)
    half = jnp.dot(
        three_center.reshape(fit_dev * block, pairs * block),
        chosen,
        preferred_element_type=jnp.float32,
    )
    half = half.astype(jnp.bfloat16).reshape(fit_dev, block, orbitals)
    terms = jnp.einsum(
        "fmi,fni->mn",
        half,
        lax.all_gather(half, "ao", axis=1, tiled=True),
        preferred_element_type=jnp.float32,
    )
    return lax.psum_scatter(terms, "fit", scatter_dimension=1, tiled=True)


def slot_sums(blocks, pair_ref, count_ref, x_ref, sums_ref, buffer, arrived, pairs_here, listed, order, counts):
    fits, block, wide = x_ref.shape
    pairs = pair_ref.shape[1]
    slots = pltpu.make_async_copy(pair_ref, pairs_here, listed)
    slots.start()
    copies = [
        pltpu.make_async_copy(x_ref.at[i], buffer.at[i, :, pl.ds(0, wide)], arrived.at[i]) for i in range(fits)
    ]
    for copy in copies:
        copy.start()
    buffer[:, :, wide:] = jnp.zeros((fits, block, block), buffer.dtype)
    z = lax.axis_index("ao")
    for place in range(blocks):
        counts[place] = 0
    slots.wait()

    def enlist(p, carry):
        place = pairs_here[0, p] ^ z
        n = counts[place]
        order[place, n] = p
        counts[place] = n + 1
        return carry

    lax.fori_loop(0, jnp.minimum(count_ref[0], pairs), enlist, 0)
    for place in range(blocks):
        n = counts[place]
        for j in range(TOGETHER - 1):
            order[place, n + j] = pairs
    for i in range(fits):
        copies[i].wait()
        for place in range(blocks):

            def slot(s):
                start = pl.multiple_of(order[place, s] * block, block)
                return buffer[i, :, pl.ds(start, block)].astype(jnp.float32)

            def add(s, total):
                s = s * TOGETHER
                return total + ((slot(s) + slot(s + 1)) + (slot(s + 2) + slot(s + 3)))

            rounds = (counts[place] + TOGETHER - 1) // TOGETHER
            whole = lax.fori_loop(0, rounds, add, jnp.zeros((block, block), jnp.float32))
            high = whole.astype(jnp.bfloat16)
            low = (whole - high.astype(jnp.float32)).astype(jnp.bfloat16)
            rows = slice(i * block, (i + 1) * block)
            sums_ref[rows, place * block : (place + 1) * block] = high
            sums_ref[rows, (blocks + place) * block : (blocks + place + 1) * block] = low


def transform(sums_ref, own_ref, third_ref, second_ref, near_ref, half_ref):
    parts = [own_ref[...], near_ref[...], second_ref[...], third_ref[...]]
    coefficients = jnp.concatenate(parts * 2, axis=0)
    half = jnp.dot(sums_ref[...], coefficients, preferred_element_type=jnp.float32)
    half_ref[...] = half.astype(jnp.bfloat16).reshape(half_ref.shape)


def blocks_sent():
    codes = []
    for targets in REDUCE:
        code = 0
        for chip, to in enumerate(targets):
            z = chip // 4
            code |= ((to % 4) ^ z if to // 4 == z else 3) << (2 * chip)
        codes.append(code - (1 << 32) if code >> 31 else code)
    return codes


def products(near, own, far, keep_ref, send_ref, whole):
    z, f = lax.axis_index("ao"), lax.axis_index("fit")
    chip, core = z * 4 + f // 2, f % 2
    columns = keep_ref.shape[1]

    def rows(ref):
        return jnp.concatenate([ref[p] for p in range(ref.shape[0])], axis=1)

    mine, next_to, beyond = rows(own), rows(near), rows(far)
    pairs = ((mine, mine), (next_to, mine), (beyond, mine), (beyond, next_to))
    for n, (left, right) in enumerate(pairs):
        whole[n] = lax.dot_general(
            left, right, (((1,), (1,)), ((), ())), preferred_element_type=jnp.float32
        )
    for m, code in enumerate(blocks_sent()):
        n = (jnp.int32(code) >> (2 * chip)) & 3
        keep_ref[m] = whole[n, pl.ds(pl.multiple_of((1 - core) * columns, columns), columns), :]
        send_ref[m] = whole[n, pl.ds(pl.multiple_of(core * columns, columns), columns), :]


def permuted_form(blocks, coefficients, three_center, pair_blocks, pair_count):
    fits, block, wide = three_center.shape
    pairs = pair_blocks.shape[1]
    orbitals = coefficients.shape[1]
    columns = block // 2

    def over_ao(x, k):
        return lax.ppermute(x, "ao", [(i, i ^ k) for i in range(blocks)])

    def over_fit(x, k):
        return lax.ppermute(x, "fit", [(i, i ^ k) for i in range(2 * blocks)])

    def held(x):
        return pltpu.with_memory_space_constraint(x, pltpu.VMEM)

    def far(x):
        return pltpu.with_memory_space_constraint(x, pltpu.HBM)

    coefs = [over_ao(coefficients, k) for k in (3, 2, 1)]
    sums = pl.pallas_call(
        functools.partial(slot_sums, blocks),
        out_shape=pltpu.VMEM((fits * block, 2 * blocks * block), jnp.bfloat16),
        in_specs=[HBM, SMEM, HBM],
        out_specs=VMEM,
        scratch_shapes=[
            pltpu.VMEM((fits, block, wide + block), jnp.bfloat16),
            pltpu.SemaphoreType.DMA((fits,)),
            pltpu.SMEM((1, pairs), jnp.int32),
            pltpu.SemaphoreType.DMA,
            pltpu.SMEM((blocks, pairs + TOGETHER), jnp.int32),
            pltpu.SMEM((blocks,), jnp.int32),
        ],
        compiler_params=pltpu.CompilerParams(vmem_limit_bytes=32 << 20),
        cost_estimate=pl.CostEstimate(
            flops=fits * block * wide, bytes_accessed=2 * fits * block * wide, transcendentals=0
        ),
        name="slot_sums",
    )(far(pair_blocks), pair_count, far(three_center))
    half = pl.pallas_call(
        transform,
        out_shape=pltpu.VMEM((fits, block, orbitals), jnp.bfloat16),
        in_specs=[VMEM] * (blocks + 1),
        out_specs=VMEM,
        name="transform",
    )(held(sums), *[held(x) for x in [coefficients] + coefs])
    near, far_rows = over_ao(half, 1), over_ao(half, 2)
    piece = pltpu.VMEM((blocks, columns, block), jnp.float32)
    keep, send = pl.pallas_call(
        products,
        out_shape=(piece, piece),
        in_specs=[VMEM] * 3,
        out_specs=(VMEM, VMEM),
        scratch_shapes=[pltpu.VMEM((blocks, block, block), jnp.float32)],
        name="products",
    )(held(near), held(half), held(far_rows))
    chip = keep + over_fit(send, 1)
    total = None
    for m, targets in enumerate(REDUCE):
        pairs = [(2 * at + c, 2 * to + 1 - c) for at, to in enumerate(targets) for c in range(2)]
        part = lax.ppermute(chip[m], ("ao", "fit"), pairs)
        total = part if total is None else total + part
    return total.T


def solution(mesh):
    blocks, fit = mesh.shape["ao"], mesh.shape["fit"]

    def per_device(coefficients, three_center, pair_blocks, pair_count):
        block = three_center.shape[1]
        fast = (
            fit == 2 * blocks
            and blocks == 4
            and block % 128 == 0
            and coefficients.shape[1] % 128 == 0
            and coefficients.shape[0] == block
            and pair_blocks.shape[0] == 1
        )
        form = functools.partial(permuted_form, blocks) if fast else gathered_form
        return form(coefficients, three_center, pair_blocks, pair_count)

    return jax.shard_map(
        per_device,
        mesh=mesh,
        in_specs=(P("ao", None), P("fit", "ao", None), P("ao", None), P("ao")),
        out_specs=P("ao", "fit"),
        check_vma=False,
    )
```

```python
import functools

import jax
import jax.numpy as jnp
from jax import lax
from jax.experimental import pallas as pl
from jax.experimental.pallas import tpu as pltpu
from jax.sharding import PartitionSpec as P

VMEM = pl.BlockSpec(memory_space=pltpu.VMEM)
HBM = pl.BlockSpec(memory_space=pltpu.HBM)
SMEM = pl.BlockSpec(memory_space=pltpu.SMEM)
TOGETHER = 4
REDUCE = (
    (0, 2, 6, 1, 4, 7, 3, 5, 12, 8, 10, 11, 13, 9, 15, 14),
    (1, 0, 2, 6, 3, 5, 4, 7, 11, 10, 12, 8, 14, 13, 9, 15),
    (6, 1, 0, 2, 5, 3, 7, 4, 10, 11, 8, 12, 15, 14, 13, 9),
    (2, 6, 1, 0, 7, 4, 5, 3, 8, 12, 11, 10, 9, 15, 14, 13),
)


def gathered_form(coefficients, three_center, pair_blocks, pair_count):
    fit_dev = three_center.shape[0]
    block = three_center.shape[1]
    pairs = pair_blocks.shape[1]
    orbitals = coefficients.shape[1]
    every = lax.all_gather(coefficients, "ao", axis=0, tiled=True)
    chosen = every.reshape(-1, block, orbitals)[pair_blocks[0]]
    live = (jnp.arange(pairs, dtype=jnp.int32) < pair_count[0])[:, None, None]
    chosen = jnp.where(live, chosen, jnp.zeros_like(chosen)).reshape(pairs * block, orbitals)
    half = jnp.dot(
        three_center.reshape(fit_dev * block, pairs * block),
        chosen,
        preferred_element_type=jnp.float32,
    )
    half = half.astype(jnp.bfloat16).reshape(fit_dev, block, orbitals)
    terms = jnp.einsum(
        "fmi,fni->mn",
        half,
        lax.all_gather(half, "ao", axis=1, tiled=True),
        preferred_element_type=jnp.float32,
    )
    return lax.psum_scatter(terms, "fit", scatter_dimension=1, tiled=True)


def slot_sums(blocks, pair_ref, count_ref, x_ref, sums_ref, buffer, arrived, pairs_here, listed, order, counts):
    fits, block, wide = x_ref.shape
    pairs = pair_ref.shape[1]
    slots = pltpu.make_async_copy(pair_ref, pairs_here, listed)
    slots.start()
    copies = [
        pltpu.make_async_copy(x_ref.at[i], buffer.at[i, :, pl.ds(0, wide)], arrived.at[i]) for i in range(fits)
    ]
    for copy in copies:
        copy.start()
    buffer[:, :, wide:] = jnp.zeros((fits, block, block), buffer.dtype)
    z = lax.axis_index("ao")
    for place in range(blocks):
        counts[place] = 0
    slots.wait()

    def enlist(p, carry):
        place = pairs_here[0, p] ^ z
        n = counts[place]
        order[place, n] = p
        counts[place] = n + 1
        return carry

    lax.fori_loop(0, jnp.minimum(count_ref[0], pairs), enlist, 0)
    for place in range(blocks):
        n = counts[place]
        for j in range(TOGETHER - 1):
            order[place, n + j] = pairs
    for i in range(fits):
        copies[i].wait()
        for place in range(blocks):

            def slot(s):
                start = pl.multiple_of(order[place, s] * block, block)
                return buffer[i, :, pl.ds(start, block)].astype(jnp.float32)

            def add(s, total):
                s = s * TOGETHER
                return total + ((slot(s) + slot(s + 1)) + (slot(s + 2) + slot(s + 3)))

            rounds = (counts[place] + TOGETHER - 1) // TOGETHER
            whole = lax.fori_loop(0, rounds, add, jnp.zeros((block, block), jnp.float32))
            high = whole.astype(jnp.bfloat16)
            low = (whole - high.astype(jnp.float32)).astype(jnp.bfloat16)
            rows = slice(i * block, (i + 1) * block)
            sums_ref[rows, place * block : (place + 1) * block] = high
            sums_ref[rows, (blocks + place) * block : (blocks + place + 1) * block] = low


def transform(sums_ref, own_ref, third_ref, second_ref, near_ref, half_ref):
    parts = [own_ref[...], near_ref[...], second_ref[...], third_ref[...]]
    coefficients = jnp.concatenate(parts * 2, axis=0)
    half = jnp.dot(sums_ref[...], coefficients, preferred_element_type=jnp.float32)
    half_ref[...] = half.astype(jnp.bfloat16).reshape(half_ref.shape)


def blocks_sent():
    codes = []
    for targets in REDUCE:
        code = 0
        for chip, to in enumerate(targets):
            z = chip // 4
            code |= ((to % 4) ^ z if to // 4 == z else 3) << (2 * chip)
        codes.append(code - (1 << 32) if code >> 31 else code)
    return codes


def products(near, far, own, keep_ref, send_ref, whole):
    z, f = lax.axis_index("ao"), lax.axis_index("fit")
    chip, core = z * 4 + f // 2, f % 2
    columns = keep_ref.shape[1]

    def rows(ref):
        return jnp.concatenate([ref[p] for p in range(ref.shape[0])], axis=1)

    mine, next_to, beyond = rows(own), rows(near), rows(far)
    pairs = ((mine, mine), (next_to, mine), (beyond, mine), (beyond, next_to))
    for n, (left, right) in enumerate(pairs):
        whole[n] = lax.dot_general(
            left, right, (((1,), (1,)), ((), ())), preferred_element_type=jnp.float32
        )
    for m, code in enumerate(blocks_sent()):
        n = (jnp.int32(code) >> (2 * chip)) & 3
        keep_ref[m] = whole[n, pl.ds(pl.multiple_of((1 - core) * columns, columns), columns), :]
        send_ref[m] = whole[n, pl.ds(pl.multiple_of(core * columns, columns), columns), :]


def permuted_form(blocks, coefficients, three_center, pair_blocks, pair_count):
    fits, block, wide = three_center.shape
    pairs = pair_blocks.shape[1]
    orbitals = coefficients.shape[1]
    columns = block // 2

    def over_ao(x, k):
        return lax.ppermute(x, "ao", [(i, i ^ k) for i in range(blocks)])

    def over_fit(x, k):
        return lax.ppermute(x, "fit", [(i, i ^ k) for i in range(2 * blocks)])

    def held(x):
        return pltpu.with_memory_space_constraint(x, pltpu.VMEM)

    def far(x):
        return pltpu.with_memory_space_constraint(x, pltpu.HBM)

    coefs = [over_ao(coefficients, k) for k in (3, 2, 1)]
    sums = pl.pallas_call(
        functools.partial(slot_sums, blocks),
        out_shape=pltpu.VMEM((fits * block, 2 * blocks * block), jnp.bfloat16),
        in_specs=[HBM, SMEM, HBM],
        out_specs=VMEM,
        scratch_shapes=[
            pltpu.VMEM((fits, block, wide + block), jnp.bfloat16),
            pltpu.SemaphoreType.DMA((fits,)),
            pltpu.SMEM((1, pairs), jnp.int32),
            pltpu.SemaphoreType.DMA,
            pltpu.SMEM((blocks, pairs + TOGETHER), jnp.int32),
            pltpu.SMEM((blocks,), jnp.int32),
        ],
        compiler_params=pltpu.CompilerParams(vmem_limit_bytes=32 << 20),
        cost_estimate=pl.CostEstimate(
            flops=fits * block * wide, bytes_accessed=2 * fits * block * wide, transcendentals=0
        ),
        name="slot_sums",
    )(far(pair_blocks), pair_count, far(three_center))
    half = pl.pallas_call(
        transform,
        out_shape=pltpu.VMEM((fits, block, orbitals), jnp.bfloat16),
        in_specs=[VMEM] * (blocks + 1),
        out_specs=VMEM,
        name="transform",
    )(held(sums), *[held(x) for x in [coefficients] + coefs])
    near, far_rows = over_ao(half, 1), over_ao(half, 2)
    piece = pltpu.VMEM((blocks, columns, block), jnp.float32)
    keep, send = pl.pallas_call(
        products,
        out_shape=(piece, piece),
        in_specs=[VMEM] * 3,
        out_specs=(VMEM, VMEM),
        scratch_shapes=[pltpu.VMEM((blocks, block, block), jnp.float32)],
        name="products",
    )(held(near), held(far_rows), held(half))
    chip = keep + over_fit(send, 1)
    total = None
    for m, targets in enumerate(REDUCE):
        pairs = [(2 * at + c, 2 * to + 1 - c) for at, to in enumerate(targets) for c in range(2)]
        part = lax.ppermute(chip[m], ("ao", "fit"), pairs)
        total = part if total is None else total + part
    return total.T


def solution(mesh):
    blocks, fit = mesh.shape["ao"], mesh.shape["fit"]

    def per_device(coefficients, three_center, pair_blocks, pair_count):
        block = three_center.shape[1]
        fast = (
            fit == 2 * blocks
            and blocks == 4
            and block % 128 == 0
            and coefficients.shape[1] % 128 == 0
            and coefficients.shape[0] == block
            and pair_blocks.shape[0] == 1
        )
        form = functools.partial(permuted_form, blocks) if fast else gathered_form
        return form(coefficients, three_center, pair_blocks, pair_count)

    return jax.shard_map(
        per_device,
        mesh=mesh,
        in_specs=(P("ao", None), P("fit", "ao", None), P("ao", None), P("ao")),
        out_specs=P("ao", "fit"),
        check_vma=False,
    )
```
